32 devices in a mesh: groups: 2 (over x), vocab: 8 (over z, y), rows: 2 (over core).
Axes of the slice: x: 2, y: 2, z: 4, core: 2. Of those that a mesh axis runs over, the one named last changes fastest.
Arguments:
- teacher_hidden: bfloat16 [256, 4608], P(('groups', 'vocab', 'rows')), parts along dimension 0, may hold values from -24 to 24
- student_hidden: bfloat16 [256, 3584], P(('groups', 'vocab', 'rows')), parts along dimension 0, may hold values from -24 to 24
- teacher_head: bfloat16 [4608, 5120], P(None, 'vocab'), may hold values from -0.09375 to 0.09375
- student_head: bfloat16 [3584, 5120], P(None, 'vocab'), may hold values from -0.09375 to 0.09375
- dest_slot: int32 [256], P(('groups', 'vocab', 'rows')), parts along dimension 0, may hold values from 0 to 15, as said below
- targets: int32 [256], P(('groups', 'vocab', 'rows')), parts along dimension 0, may hold values from 0 to 5119
- token_grad: bfloat16 [256], P(('groups', 'vocab', 'rows')), parts along dimension 0, may hold values from 50 to 500
Outputs:
- token_loss: float32 [256], P(('groups', 'vocab', 'rows')), parts along dimension 0
- hidden_grad: bfloat16 [256, 3584], P(('groups', 'vocab', 'rows')), parts along dimension 0
The draws below stay inside these ranges and needn't reach their ends.
There are 2 independent parts, one for each index of `groups`. The reference program is written for one: setup_inputs(seed, part) draws one part's arguments, and reference() takes and returns one part's arrays. A program takes and returns all parts, laid end to end along the dimension named above; an argument that names none is the same for every part. Nothing has to cross between parts.
Inputs may be any that keep to these rules, and one draw needn't show every extreme that they name: Within each pair block of 16 consecutive rows, dest_slot is a permutation of 0 to 15.
All inputs are finite; a program needn't handle non-finite values.
Results may differ from the reference program's by a relative error of at most 0.0048.
Values may be sent and summed in bfloat16 or wider, within the bound.
A program may use at most 64 MiB of HBM per device.

```python
import math
import jax
import jax.numpy as jnp
import numpy as np
from jax import lax

DT = 4608
DS = 3584
TOK_DEV = 8
VOCAB = 5120
TOKENS = 128
N_VOCAB = 8
N_ROWS = 2


def draw_dest_slot(key, part):
    key = jax.random.fold_in(key, 11)
    span = N_ROWS * TOK_DEV
    keys = jax.random.split(key, N_VOCAB)
    orders = jax.vmap(lambda one_key: jax.random.permutation(one_key, span))(keys)
    return orders.reshape(-1).astype(jnp.int32)


def plant(array, stream_key, least, top_value):
    longest = array.shape.index(max(array.shape))
    spots = []
    for shift in (0, 1):
        where = [jax.random.randint(jax.random.fold_in(stream_key, axis), (), 0, length) for axis, length in enumerate(array.shape)]
        where[longest] = (where[longest] + shift) % array.shape[longest]
        spots.append(tuple(where))
    return array.at[spots[0]].set(least).at[spots[1]].set(top_value)


def block_scale(rng, dims, shards, low, high):
    level, own = 1.0, jax.random.fold_in(rng, 6)
    for axis_at, parts in shards:
        draws = jnp.exp(jax.random.uniform(jax.random.fold_in(own, axis_at), (parts,), jnp.float32, low / len(shards), high / len(shards)))
        level = level * jnp.repeat(draws, dims[axis_at] // parts).reshape([-1 if axis == axis_at else 1 for axis in range(len(dims))])
    return level


def rank_bounds(number_of, skew):
    loads = [(1 << 20) // math.isqrt(standing ** skew) + 1 for standing in range(1, number_of + 1)]
    scale = 1 + sum(loads) // (1 << 30)
    return np.cumsum(np.array([max(1, weight // scale) for weight in loads]))


def ranked_ids(stream_key, dims, amount, skew):
    listing = rank_bounds(amount, skew)
    lot = jax.random.randint(jax.random.fold_in(stream_key, 1), dims, 0, int(listing[amount - 1]))
    standing = jnp.searchsorted(jnp.asarray(listing, jnp.int32), lot, side="right")
    return jax.random.permutation(jax.random.fold_in(stream_key, 2), amount)[standing].astype(jnp.int32)


def noise(own_key, dims, scale, reach, cuts=(), kind=jnp.bfloat16):
    loudness = block_scale(own_key, dims, cuts, -0.22, 0.18) if cuts else 1.0
    values = jax.random.normal(own_key, dims, jnp.float32) * scale * loudness
    return jnp.minimum(jnp.maximum(values, -reach), reach).astype(kind)


def setup_inputs(seed: int = 0, part: int = 0) -> dict:
    splits = jax.random.split(jax.random.key(seed), 8)
    part_splits = jax.random.split(jax.random.fold_in(splits[7], part), 8)
    teacher_hidden = noise(part_splits[0], (TOKENS, DT), 4.0, 24.0, ((0, 16),))
    student_hidden = noise(part_splits[1], (TOKENS, DS), 4.0, 24.0, ((0, 16),))
    teacher_head = noise(splits[2], (DT, VOCAB), DT ** -0.5, 0.09375, ((1, 8),))
    student_head = noise(splits[3], (DS, VOCAB), DS ** -0.5, 0.09375, ((1, 8),))
    dest_slot = draw_dest_slot(jax.random.fold_in(jax.random.fold_in(splits[7], part), 71), part)
    targets = plant(ranked_ids(part_splits[5], (TOKENS,), VOCAB, 2), jax.random.fold_in(part_splits[5], 3), 0, VOCAB - 1).astype(jnp.int32)
    token_grad = jnp.clip(jnp.exp(math.log(500.0) - 2.3025851 * jax.random.uniform(part_splits[6], (TOKENS,), jnp.float32) ** block_scale(part_splits[6], (TOKENS,), ((0, 16),), -0.2, 0.2)), 50.0, 500.0).astype(jnp.bfloat16)
    return dict(teacher_hidden=teacher_hidden, student_hidden=student_hidden, teacher_head=teacher_head, student_head=student_head, dest_slot=dest_slot, targets=targets, token_grad=token_grad)


soft_cap = 30.0


def capped(values):
    return soft_cap * jnp.tanh(values / soft_cap)


def reference(teacher_hidden, student_hidden, teacher_head, student_head, dest_slot, targets, token_grad):
    span = N_ROWS * TOK_DEV
    starts = (jnp.arange(TOKENS, dtype=jnp.int32) // span) * span
    aligned = jnp.zeros_like(teacher_hidden).at[(starts + dest_slot).astype(jnp.int32)].set(teacher_hidden)
    blocks = TOKENS // TOK_DEV
    columns = jnp.arange(VOCAB, dtype=jnp.int32)

    def one_block(pieces):
        teach, stud, target_ids, weight = pieces
        logit_t = capped(jnp.dot(teach, teacher_head, preferred_element_type=jnp.float32))
        logit_s = capped(jnp.dot(stud, student_head, preferred_element_type=jnp.float32))
        exp_t = jnp.exp(logit_t)
        exp_s = jnp.exp(logit_s)
        norm_t = jnp.sum(exp_t, axis=1)
        cross = jnp.sum(exp_t * (logit_t - logit_s), axis=1)
        norm_s = jnp.sum(exp_s, axis=1)
        onehot = target_ids[:, None] == columns[None, :]
        hit = jnp.sum(jnp.where(onehot, logit_s, 0.0), axis=1)
        loss = cross / norm_t - jnp.log(norm_t) + 2.0 * jnp.log(norm_s) - hit
        slope = 1.0 - (logit_s / soft_cap) * (logit_s / soft_cap)
        grad = weight.astype(jnp.float32)[:, None] * (2.0 * exp_s / norm_s[:, None] - exp_t / norm_t[:, None] - onehot.astype(jnp.float32)) * slope
        grad = grad.astype(jnp.bfloat16)
        back = lax.dot_general(grad, student_head, (((1,), (1,)), ((), ())), preferred_element_type=jnp.float32)
        return loss, back.astype(jnp.bfloat16)

    loss, back = lax.map(one_block, (aligned.reshape(blocks, TOK_DEV, DT), student_hidden.reshape(blocks, TOK_DEV, DS), targets.reshape(blocks, TOK_DEV), token_grad.reshape(blocks, TOK_DEV)))
    return loss.reshape(TOKENS), back.reshape(TOKENS, DS)
```

```python
import functools

import jax
import jax.numpy as jnp
from jax import lax
from jax.experimental import pallas as pl
from jax.experimental.pallas import tpu as pltpu
from jax.sharding import PartitionSpec as P

soft_cap = 30.0
CHUNKS = 4
BACK = 2
F32 = jnp.float32
BF16 = jnp.bfloat16


def capped(values):
    return soft_cap * jnp.tanh(values / soft_cap)


def iota(shape, dim):
    return lax.broadcasted_iota(jnp.int32, shape, dim)


def to_row(column):
    size = column.shape[0]
    eye = iota((size, size), 0) == iota((size, size), 1)
    return jnp.sum(jnp.where(eye, column, 0.0), axis=0, keepdims=True)


def to_column(row):
    size = row.shape[1]
    eye = iota((size, size), 0) == iota((size, size), 1)
    return jnp.sum(jnp.where(eye, row, 0.0), axis=1, keepdims=True)


def stacked(values):
    half = values.shape[1] // 2
    return jnp.concatenate([values[:, :half], values[:, half:]], axis=0)


def kernel(
    far, near,
    th_ref, sh_ref, dest_ref, target_ref, weight_ref, thead_ref, shead_ref,
    loss_ref, hidden_ref,
    heads, swap_out, swap_in, blocks, meta, stats, lt, ls, back_out, back_in,
    head_sem, swap_sem, arrive, up_sem, down_sem, side_sem,
    meta_send, meta_recv, stat_send, stat_recv, back_send, back_recv,
):
    n = far * near
    rows, wide_t = th_ref.shape
    wide_s = sh_ref.shape[1]
    half = (wide_t + wide_s) // 2
    chunk = half // CHUNKS
    shard = heads.shape[1]
    tokens = n * rows
    v = lax.axis_index("vocab")
    r = lax.axis_index("rows")
    z, y = lax.div(v, near), lax.rem(v, near)

    loads = [
        pltpu.make_async_copy(thead_ref, heads.at[pl.ds(0, wide_t)], head_sem.at[0]),
        pltpu.make_async_copy(shead_ref, heads.at[pl.ds(wide_t, wide_s)], head_sem.at[1]),
    ]
    for load in loads:
        load.start()

    barrier = pltpu.get_barrier_semaphore()
    pl.semaphore_signal(barrier, inc=1, device_id={"rows": 1 - r})
    for step in range(1, n):
        pl.semaphore_signal(barrier, inc=1, device_id={"vocab": lax.rem(v + step, n)})

    lanes = iota((rows, rows), 1)
    place = iota((rows, rows), 0)
    slots = jnp.zeros((rows, rows), jnp.int32)
    for j in range(rows):
        slots = jnp.where(lanes == j, dest_ref[j], slots)
    teacher = th_ref[...]

    def picked(core):
        chosen = jnp.where(slots == core * rows + place, 1.0, 0.0).astype(BF16)
        return jnp.dot(chosen, teacher, preferred_element_type=F32)

    swap_out[...] = stacked(picked(1 - r)).astype(BF16)
    row_at = iota((rows, 128), 0)
    lane_at = iota((rows, 128), 1)
    own_meta = jnp.where(
        lane_at == 1, to_column(weight_ref[...].astype(F32).reshape(1, rows)), 0.0
    )
    for j in range(rows):
        own_meta = jnp.where((lane_at == 0) & (row_at == j), target_ref[j].astype(F32), own_meta)
    meta[v] = own_meta
    kept = picked(r)
    pl.semaphore_wait(barrier, n)

    swap = pltpu.make_async_remote_copy(
        swap_out, swap_in, swap_sem.at[0], swap_sem.at[1], device_id={"rows": 1 - r}
    )
    swap.start()

    def to_all(src, dst, sends, recvs):
        copies = []
        for step in range(1, n):
            copies.append(
                pltpu.make_async_remote_copy(
                    src, dst, sends.at[step - 1], recvs.at[step - 1],
                    device_id={"vocab": lax.rem(v + step, n)},
                )
            )
            copies[-1].start()
        return copies

    meta_copies = to_all(meta.at[v], meta.at[v], meta_send, meta_recv)
    swap.wait_recv()
    moved = swap_in[...].astype(F32)
    aligned = kept + jnp.concatenate([moved[:rows], moved[rows:]], axis=1)
    own = stacked(jnp.concatenate([aligned, sh_ref[...].astype(F32)], axis=1))
    blocks[v] = own.astype(BF16)

    def piece(source, c):
        return blocks.at[source, :, pl.ds(c * chunk, chunk)]

    def vertical(source, c, up):
        source_z = lax.div(source, near)
        sems = up_sem if up else down_sem
        return pltpu.make_async_remote_copy(
            piece(source, c), piece(source, c), sems.at[source_z, c], arrive.at[source, c],
            device_id={"vocab": v + near if up else v - near},
        )

    def sideways(source, c, step):
        source_z = lax.div(source, near)
        return pltpu.make_async_remote_copy(
            piece(source, c), piece(source, c), side_sem.at[step - 1, source_z, c],
            arrive.at[source, c],
            device_id={"vocab": z * near + lax.rem(y + step, near)},
        )

    def spread(source, c, up, down):
        if up:
            @pl.when(z < far - 1)
            def _():
                vertical(source, c, True).start()
        if down:
            @pl.when(z > 0)
            def _():
                vertical(source, c, False).start()
        for step in range(1, near):
            sideways(source, c, step).start()

    def product(c):
        both = blocks[:, :, c * chunk:(c + 1) * chunk].astype(F32)
        for part in range(2):
            x = both[:, part * rows:(part + 1) * rows].reshape(tokens, chunk).astype(BF16)
            first = part * half + c * chunk
            for out, begin, end in ((lt, 0, wide_t), (ls, wide_t, wide_t + wide_s)):
                low, high = max(first, begin), min(first + chunk, end)
                if low < high:
                    out[...] += jnp.dot(
                        x[:, low - first:high - first], heads[low:high, :],
                        preferred_element_type=F32,
                    )

    lt[...] = jnp.zeros_like(lt)
    ls[...] = jnp.zeros_like(ls)
    spread(v, 0, True, True)
    for t in range(CHUNKS + far):
        if t + 1 < CHUNKS:
            spread(v, t + 1, True, True)
        for d in range(1, far):
            c = t - d
            if 0 <= c < CHUNKS:
                @pl.when(z >= d)
                def _():
                    vertical(v - d * near, c, True).wait_recv()
                    spread(v - d * near, c, True, False)

                @pl.when(z + d < far)
                def _():
                    vertical(v + d * near, c, False).wait_recv()
                    spread(v + d * near, c, False, True)
        c = t - far
        if c >= 0:
            for step in range(1, near):
                for source_z in range(far):
                    source = source_z * near + lax.rem(y + step, near)
                    sideways(source, c, step).wait_recv()
            if c == 0:
                for load in loads:
                    load.wait()
            product(c)
    for copy in meta_copies:
        copy.wait_recv()

    info = meta[...].reshape(tokens, 128)
    target = info[:, 0:1].astype(jnp.int32) - v * shard
    weight = info[:, 1:2]
    onehot = iota((tokens, shard), 1) == target
    logit_t = capped(lt[...])
    exp_t = jnp.exp(logit_t)
    logit_s = capped(ls[...])
    exp_s = jnp.exp(logit_s)
    sums = (
        jnp.sum(exp_t, axis=1, keepdims=True),
        jnp.sum(exp_t * (logit_t - logit_s), axis=1, keepdims=True),
        jnp.sum(exp_s, axis=1, keepdims=True),
        jnp.sum(jnp.where(onehot, logit_s, 0.0), axis=1, keepdims=True),
    )
    stat_row = iota((8, tokens), 0)
    mine = jnp.zeros((8, tokens), F32)
    for k, column in enumerate(sums):
        mine = jnp.where(stat_row == k, to_row(column), mine)
    stats[v] = mine
    stat_copies = to_all(stats.at[v], stats.at[v], stat_send, stat_recv)
    slope = 1.0 - (logit_s / soft_cap) * (logit_s / soft_cap)
    for copy in stat_copies:
        copy.wait_recv()
    total = jnp.sum(stats[...], axis=0)
    norm_t, cross, norm_s, hit = (total[k:k + 1] for k in range(4))
    zt, zs = to_column(norm_t), to_column(norm_s)
    grad = (
        weight
        * (exp_s * (2.0 / zs) - exp_t * (1.0 / zt) - jnp.where(onehot, 1.0, 0.0))
        * slope
    ).astype(BF16)

    cols = wide_s // 2 // BACK

    def backed(q, part):
        first = wide_t + part * (wide_s // 2) + q * cols
        return lax.dot_general(
            grad, heads[first:first + cols, :], (((1,), (1,)), ((), ())),
            preferred_element_type=F32,
        ).astype(BF16).astype(F32).reshape(n, rows, cols)

    back_copies = []
    for q in range(BACK):
        joined = jnp.concatenate([backed(q, 0), backed(q, 1)], axis=1)
        back_out[:, q] = joined.astype(BF16)
        for step in range(1, n):
            there = lax.rem(v + step, n)
            back_copies.append(
                pltpu.make_async_remote_copy(
                    back_out.at[there, q], back_in.at[step - 1, q],
                    back_send.at[step - 1, q], back_recv.at[step - 1, q],
                    device_id={"vocab": there},
                )
            )
            back_copies[-1].start()

    loss = cross / norm_t - jnp.log(norm_t) + 2.0 * jnp.log(norm_s) - hit
    choose = iota((rows, tokens), 1) == v * rows + iota((rows, tokens), 0)
    loss_ref[...] = to_row(jnp.sum(jnp.where(choose, loss, 0.0), axis=1, keepdims=True))

    k = 0
    for q in range(BACK):
        result = back_out[v, q].astype(F32)
        for step in range(1, n):
            back_copies[k].wait_recv()
            k += 1
            result += back_in[step - 1, q].astype(F32)
        result = jnp.concatenate([result[:rows], result[rows:]], axis=1).astype(BF16)
        hidden_ref[:, q * cols:(q + 1) * cols] = result[:, :cols]
        hidden_ref[:, wide_s // 2 + q * cols:wide_s // 2 + (q + 1) * cols] = result[:, cols:]

    swap.wait_send()
    for copy in meta_copies + stat_copies + back_copies:
        copy.wait_send()
    for c in range(CHUNKS):
        for d in range(far):
            @pl.when((z >= d) & (z < far - 1))
            def _():
                vertical(v - d * near, c, True).wait_send()

            @pl.when((z + d < far) & (z > 0))
            def _():
                vertical(v + d * near, c, False).wait_send()
        for source_z in range(far):
            for step in range(1, near):
                sideways(source_z * near + y, c, step).wait_send()


def local(far, near, teacher_hidden, student_hidden, teacher_head, student_head, dest_slot, targets, token_grad):
    n = far * near
    rows, wide_t = teacher_hidden.shape
    wide_s = student_hidden.shape[1]
    shard = student_head.shape[1]
    tokens = n * rows
    half = (wide_t + wide_s) // 2
    vmem = pl.BlockSpec(memory_space=pltpu.VMEM)
    smem = pl.BlockSpec(memory_space=pltpu.SMEM)
    hbm = pl.BlockSpec(memory_space=pl.ANY)
    dma = pltpu.SemaphoreType.DMA
    loss, hidden = pl.pallas_call(
        functools.partial(kernel, far, near),
        out_shape=(
            jax.ShapeDtypeStruct((1, rows), F32),
            jax.ShapeDtypeStruct((rows, wide_s), BF16),
        ),
        in_specs=[vmem, vmem, smem, smem, vmem, hbm, hbm],
        out_specs=(vmem, vmem),
        scratch_shapes=[
            pltpu.VMEM((wide_t + wide_s, shard), BF16),
            pltpu.VMEM((2 * rows, wide_t // 2), BF16),
            pltpu.VMEM((2 * rows, wide_t // 2), BF16),
            pltpu.VMEM((n, 2 * rows, half), BF16),
            pltpu.VMEM((n, rows, 128), F32),
            pltpu.VMEM((n, 8, tokens), F32),
            pltpu.VMEM((tokens, shard), F32),
            pltpu.VMEM((tokens, shard), F32),
            pltpu.VMEM((n, BACK, 2 * rows, wide_s // 2 // BACK), BF16),
            pltpu.VMEM((n - 1, BACK, 2 * rows, wide_s // 2 // BACK), BF16),
            dma((2,)),
            dma((2,)),
            dma((n, CHUNKS)),
            dma((far, CHUNKS)),
            dma((far, CHUNKS)),
            dma((near - 1, far, CHUNKS)),
            dma((n - 1,)),
            dma((n - 1,)),
            dma((n - 1,)),
            dma((n - 1,)),
            dma((n - 1, BACK)),
            dma((n - 1, BACK)),
        ],
        compiler_params=pltpu.CompilerParams(
            collective_id=0, has_side_effects=True, vmem_limit_bytes=56 * 2**20
        ),
    )(teacher_hidden, student_hidden, dest_slot, targets, token_grad, teacher_head, student_head)
    return loss.reshape(rows), hidden


def solution(mesh):
    n = mesh.shape["vocab"]
    near = 1 << ((n.bit_length() - 1) // 2)
    far = n // near
    by_token = P(("groups", "vocab", "rows"))
    by_row = P(("groups", "vocab", "rows"), None)
    by_vocab = P(None, "vocab")
    return jax.shard_map(
        functools.partial(local, far, near),
        mesh=mesh,
        in_specs=(by_row, by_row, by_vocab, by_vocab, by_token, by_token, by_token),
        out_specs=(by_token, by_row),
        check_vma=False,
    )
```

```python
import functools

import jax
import jax.numpy as jnp
from jax import lax
from jax.experimental import pallas as pl
from jax.experimental.pallas import tpu as pltpu
from jax.sharding import PartitionSpec as P

soft_cap = 30.0
CHUNKS = 2
BACK = 1
F32 = jnp.float32
BF16 = jnp.bfloat16


def capped(values):
    return soft_cap * jnp.tanh(values / soft_cap)


def iota(shape, dim):
    return lax.broadcasted_iota(jnp.int32, shape, dim)


def to_row(column):
    size = column.shape[0]
    eye = iota((size, size), 0) == iota((size, size), 1)
    return jnp.sum(jnp.where(eye, column, 0.0), axis=0, keepdims=True)


def to_column(row):
    size = row.shape[1]
    eye = iota((size, size), 0) == iota((size, size), 1)
    return jnp.sum(jnp.where(eye, row, 0.0), axis=1, keepdims=True)


def stacked(values):
    half = values.shape[1] // 2
    return jnp.concatenate([values[:, :half], values[:, half:]], axis=0)


def kernel(
    far, near,
    th_in, sh_in, dest_in, target_in, weight_ref, thead_ref, shead_ref,
    loss_ref, hidden_ref,
    th_ref, sh_ref, dest_ref, target_ref, heads, swap_out, swap_in, blocks, stats, lt, ls, back_out, back_in,
    small_sem, head_sem, swap_sem, arrive, up_sem, down_sem, side_sem,
    stat_send, stat_recv, back_send, back_recv,
):
    n = far * near
    rows, wide_t = th_ref.shape
    wide_s = sh_ref.shape[1]
    half = (wide_t + wide_s) // 2
    chunk = half // CHUNKS
    shard = heads.shape[1]
    tokens = n * rows
    v = lax.axis_index("vocab")
    r = lax.axis_index("rows")
    z, y = lax.div(v, near), lax.rem(v, near)

    barrier = pltpu.get_barrier_semaphore()
    pl.semaphore_signal(barrier, inc=1, device_id={"rows": 1 - r})
    for step in range(1, n):
        pl.semaphore_signal(barrier, inc=1, device_id={"vocab": lax.rem(v + step, n)})

    small = [
        pltpu.make_async_copy(src, dst, small_sem.at[at])
        for at, (src, dst) in enumerate(
            ((th_in, th_ref), (dest_in, dest_ref), (target_in, target_ref), (sh_in, sh_ref))
        )
    ]
    for load in small:
        load.start()
    loads = [
        pltpu.make_async_copy(thead_ref, heads.at[pl.ds(0, wide_t)], head_sem.at[0]),
        pltpu.make_async_copy(shead_ref, heads.at[pl.ds(wide_t, wide_s)], head_sem.at[1]),
    ]
    for load in loads:
        load.start()

    for load in small:
        load.wait()

    lanes = iota((rows, rows), 1)
    place = iota((rows, rows), 0)
    slots = jnp.zeros((rows, rows), jnp.int32)
    for j in range(rows):
        slots = jnp.where(lanes == j, dest_ref[j], slots)
    teacher = th_ref[...]

    def picked(core):
        chosen = jnp.where(slots == core * rows + place, 1.0, 0.0).astype(BF16)
        return jnp.dot(chosen, teacher, preferred_element_type=F32)

    swap_out[...] = stacked(picked(1 - r)).astype(BF16)
    row_at = iota((rows, 128), 0)
    lane_at = iota((rows, 128), 1)
    own_meta = jnp.where(
        lane_at == 2, to_column(weight_ref[...].astype(F32).reshape(1, rows)), 0.0
    )
    for j in range(rows):
        own_meta = jnp.where(
            (row_at == j) & (lane_at == 0), lax.div(target_ref[j], 256).astype(F32),
            jnp.where(
                (row_at == j) & (lane_at == 1), lax.rem(target_ref[j], 256).astype(F32), own_meta
            ),
        )
    kept = picked(r)
    pl.semaphore_wait(barrier, n)

    swap = pltpu.make_async_remote_copy(
        swap_out, swap_in, swap_sem.at[0], swap_sem.at[1], device_id={"rows": 1 - r}
    )
    swap.start()

    def to_all(src, dst, sends, recvs):
        copies = []
        for step in range(1, n):
            copies.append(
                pltpu.make_async_remote_copy(
                    src, dst, sends.at[step - 1], recvs.at[step - 1],
                    device_id={"vocab": lax.rem(v + step, n)},
                )
            )
            copies[-1].start()
        return copies

    swap.wait_recv()
    moved = swap_in[...].astype(F32)
    aligned = kept + jnp.concatenate([moved[:rows], moved[rows:]], axis=1)
    own = stacked(jnp.concatenate([aligned, sh_ref[...].astype(F32)], axis=1))
    blocks[v, :, :half] = own.astype(BF16)
    blocks[v, :, half:] = jnp.concatenate([own_meta, jnp.zeros_like(own_meta)], axis=0).astype(BF16)

    def piece(source, c):
        return blocks.at[source, :, pl.ds(c * chunk, chunk + 128 if c == CHUNKS - 1 else chunk)]

    def vertical(source, c, up):
        source_z = lax.div(source, near)
        sems = up_sem if up else down_sem
        return pltpu.make_async_remote_copy(
            piece(source, c), piece(source, c), sems.at[source_z, c], arrive.at[source, c],
            device_id={"vocab": v + near if up else v - near},
        )

    def sideways(source, c, step):
        source_z = lax.div(source, near)
        return pltpu.make_async_remote_copy(
            piece(source, c), piece(source, c), side_sem.at[step - 1, source_z, c],
            arrive.at[source, c],
            device_id={"vocab": z * near + lax.rem(y + step, near)},
        )

    def spread(source, c, up, down):
        if up:
            @pl.when(z < far - 1)
            def _():
                vertical(source, c, True).start()
        if down:
            @pl.when(z > 0)
            def _():
                vertical(source, c, False).start()
        for step in range(1, near):
            sideways(source, c, step).start()

    def product(c):
        both = blocks[:, :, c * chunk:(c + 1) * chunk].astype(F32)
        for part in range(2):
            x = both[:, part * rows:(part + 1) * rows].reshape(tokens, chunk).astype(BF16)
            first = part * half + c * chunk
            for out, begin, end in ((lt, 0, wide_t), (ls, wide_t, wide_t + wide_s)):
                low, high = max(first, begin), min(first + chunk, end)
                if low < high:
                    out[...] += jnp.dot(
                        x[:, low - first:high - first], heads[low:high, :],
                        preferred_element_type=F32,
                    )

    lt[...] = jnp.zeros_like(lt)
    ls[...] = jnp.zeros_like(ls)
    spread(v, 0, True, True)
    for t in range(CHUNKS + far):
        if t == 0:
            for c in range(1, CHUNKS):
                spread(v, c, True, True)
        for d in range(1, far):
            c = t - d
            if 0 <= c < CHUNKS:
                @pl.when(z >= d)
                def _():
                    vertical(v - d * near, c, True).wait_recv()
                    spread(v - d * near, c, True, False)

                @pl.when(z + d < far)
                def _():
                    vertical(v + d * near, c, False).wait_recv()
                    spread(v + d * near, c, False, True)
        c = t - far
        if c >= 0:
            for step in range(1, near):
                for source_z in range(far):
                    source = source_z * near + lax.rem(y + step, near)
                    sideways(source, c, step).wait_recv()
            if c == 0:
                for load in loads:
                    load.wait()
            product(c)

    info = blocks[:, :, half:].astype(F32)[:, :rows].reshape(tokens, 128)
    target = (info[:, 0:1] * 256.0 + info[:, 1:2]).astype(jnp.int32) - v * shard
    weight = info[:, 2:3]
    onehot = iota((tokens, shard), 1) == target
    logit_t = capped(lt[...])
    exp_t = jnp.exp(logit_t)
    logit_s = capped(ls[...])
    exp_s = jnp.exp(logit_s)
    sums = (
        jnp.sum(exp_t, axis=1, keepdims=True),
        jnp.sum(exp_t * (logit_t - logit_s), axis=1, keepdims=True),
        jnp.sum(exp_s, axis=1, keepdims=True),
        jnp.sum(jnp.where(onehot, logit_s, 0.0), axis=1, keepdims=True),
    )
    stat_row = iota((8, tokens), 0)
    mine = jnp.zeros((8, tokens), F32)
    for k, column in enumerate(sums):
        mine = jnp.where(stat_row == k, to_row(column), mine)
    stats[v] = mine
    stat_copies = to_all(stats.at[v], stats.at[v], stat_send, stat_recv)
    slope = 1.0 - (logit_s / soft_cap) * (logit_s / soft_cap)
    for copy in stat_copies:
        copy.wait_recv()
    total = jnp.sum(stats[...], axis=0)
    norm_t, cross, norm_s, hit = (total[k:k + 1] for k in range(4))
    zt, zs = to_column(norm_t), to_column(norm_s)
    grad = (
        weight
        * (exp_s * (2.0 / zs) - exp_t * (1.0 / zt) - jnp.where(onehot, 1.0, 0.0))
        * slope
    ).astype(BF16)

    cols = wide_s // 2 // BACK

    def backed(q, part):
        first = wide_t + part * (wide_s // 2) + q * cols
        return lax.dot_general(
            grad, heads[first:first + cols, :], (((1,), (1,)), ((), ())),
            preferred_element_type=F32,
        ).astype(BF16).astype(F32).reshape(n, rows, cols)

    back_copies = []
    for q in range(BACK):
        joined = jnp.concatenate([backed(q, 0), backed(q, 1)], axis=1)
        back_out[:, q] = joined.astype(BF16)
        for step in range(1, n):
            there = lax.rem(v + step, n)
            back_copies.append(
                pltpu.make_async_remote_copy(
                    back_out.at[there, q], back_in.at[step - 1, q],
                    back_send.at[step - 1, q], back_recv.at[step - 1, q],
                    device_id={"vocab": there},
                )
            )
            back_copies[-1].start()

    loss = cross / norm_t - jnp.log(norm_t) + 2.0 * jnp.log(norm_s) - hit
    choose = iota((rows, tokens), 1) == v * rows + iota((rows, tokens), 0)
    loss_ref[...] = to_row(jnp.sum(jnp.where(choose, loss, 0.0), axis=1, keepdims=True))

    k = 0
    for q in range(BACK):
        result = back_out[v, q].astype(F32)
        for step in range(1, n):
            back_copies[k].wait_recv()
            k += 1
            result += back_in[step - 1, q].astype(F32)
        result = jnp.concatenate([result[:rows], result[rows:]], axis=1).astype(BF16)
        hidden_ref[:, q * cols:(q + 1) * cols] = result[:, :cols]
        hidden_ref[:, wide_s // 2 + q * cols:wide_s // 2 + (q + 1) * cols] = result[:, cols:]

    swap.wait_send()
    for copy in stat_copies + back_copies:
        copy.wait_send()
    for c in range(CHUNKS):
        for d in range(far):
            @pl.when((z >= d) & (z < far - 1))
            def _():
                vertical(v - d * near, c, True).wait_send()

            @pl.when((z + d < far) & (z > 0))
            def _():
                vertical(v + d * near, c, False).wait_send()
        for source_z in range(far):
            for step in range(1, near):
                sideways(source_z * near + y, c, step).wait_send()


def hand_on(loss_in, hidden_in, loss_ref, hidden_ref):
    loss_ref[...] = loss_in[...]
    hidden_ref[...] = hidden_in[...]


def local(far, near, teacher_hidden, student_hidden, teacher_head, student_head, dest_slot, targets, token_grad):
    n = far * near
    rows, wide_t = teacher_hidden.shape
    wide_s = student_hidden.shape[1]
    shard = student_head.shape[1]
    tokens = n * rows
    half = (wide_t + wide_s) // 2
    vmem = pl.BlockSpec(memory_space=pltpu.VMEM)
    hbm = pl.BlockSpec(memory_space=pl.ANY)
    dma = pltpu.SemaphoreType.DMA
    loss, hidden = pl.pallas_call(
        functools.partial(kernel, far, near),
        out_shape=(
            jax.ShapeDtypeStruct((1, rows), F32),
            jax.ShapeDtypeStruct((rows, wide_s), BF16),
        ),
        in_specs=[hbm, hbm, hbm, hbm, vmem, hbm, hbm],
        out_specs=(vmem, vmem),
        scratch_shapes=[
            pltpu.VMEM((rows, wide_t), BF16),
            pltpu.VMEM((rows, wide_s), BF16),
            pltpu.SMEM((rows,), jnp.int32),
            pltpu.SMEM((rows,), jnp.int32),
            pltpu.VMEM((wide_t + wide_s, shard), BF16),
            pltpu.VMEM((2 * rows, wide_t // 2), BF16),
            pltpu.VMEM((2 * rows, wide_t // 2), BF16),
            pltpu.VMEM((n, 2 * rows, half + 128), BF16),
            pltpu.VMEM((n, 8, tokens), F32),
            pltpu.VMEM((tokens, shard), F32),
            pltpu.VMEM((tokens, shard), F32),
            pltpu.VMEM((n, BACK, 2 * rows, wide_s // 2 // BACK), BF16),
            pltpu.VMEM((n - 1, BACK, 2 * rows, wide_s // 2 // BACK), BF16),
            dma((4,)),
            dma((2,)),
            dma((2,)),
            dma((n, CHUNKS)),
            dma((far, CHUNKS)),
            dma((far, CHUNKS)),
            dma((near - 1, far, CHUNKS)),
            dma((n - 1,)),
            dma((n - 1,)),
            dma((n - 1, BACK)),
            dma((n - 1, BACK)),
        ],
        compiler_params=pltpu.CompilerParams(
            collective_id=0, has_side_effects=True, vmem_limit_bytes=56 * 2**20
        ),
    )(teacher_hidden, student_hidden, dest_slot, targets, token_grad, teacher_head, student_head)
    loss, hidden = pl.pallas_call(
        hand_on,
        out_shape=(jax.ShapeDtypeStruct((1, rows), F32), jax.ShapeDtypeStruct((rows, wide_s), BF16)),
        in_specs=[vmem, vmem],
        out_specs=(vmem, vmem),
    )(loss, hidden)
    return loss.reshape(rows), hidden


def solution(mesh):
    n = mesh.shape["vocab"]
    near = 1 << ((n.bit_length() - 1) // 2)
    far = n // near
    by_token = P(("groups", "vocab", "rows"))
    by_row = P(("groups", "vocab", "rows"), None)
    by_vocab = P(None, "vocab")
    return jax.shard_map(
        functools.partial(local, far, near),
        mesh=mesh,
        in_specs=(by_row, by_row, by_vocab, by_vocab, by_token, by_token, by_token),
        out_specs=(by_token, by_row),
        check_vma=False,
    )
```

```python
import functools

import jax
import jax.numpy as jnp
from jax import lax
from jax.experimental import pallas as pl
from jax.experimental.pallas import tpu as pltpu
from jax.sharding import PartitionSpec as P

soft_cap = 30.0
CROSS = 768
BACK = 1
F32 = jnp.float32
BF16 = jnp.bfloat16


def capped(values):
    return soft_cap * jnp.tanh(values / soft_cap)


def iota(shape, dim):
    return lax.broadcasted_iota(jnp.int32, shape, dim)


def to_row(column):
    size = column.shape[0]
    eye = iota((size, size), 0) == iota((size, size), 1)
    return jnp.sum(jnp.where(eye, column, 0.0), axis=0, keepdims=True)


def to_column(row):
    size = row.shape[1]
    eye = iota((size, size), 0) == iota((size, size), 1)
    return jnp.sum(jnp.where(eye, row, 0.0), axis=1, keepdims=True)


def stacked(values):
    half = values.shape[1] // 2
    return jnp.concatenate([values[:, :half], values[:, half:]], axis=0)


def kernel(
    far, near,
    th_in, sh_in, dest_in, target_in, weight_ref, thead_ref, shead_ref,
    loss_ref, hidden_ref,
    th_ref, sh_ref, dest_ref, target_ref, heads, swap_out, swap_in, blocks, stats, lt, ls, back_out, back_in,
    small_sem, head_sem, swap_sem, arrive, up_sem, down_sem, side_sem,
    stat_send, stat_recv, back_send, back_recv,
):
    n = far * near
    rows, wide_t = th_ref.shape
    wide_s = sh_ref.shape[1]
    half_s, half_t = wide_s // 2, wide_t // 2
    gap = half_s + 128
    kept_t = half_t - CROSS
    chunks = [
        (0, gap, half_s, ls, (wide_t, wide_t + half_s), False),
        (gap, kept_t, kept_t, lt, (0, half_t), False),
    ]
    if CROSS:
        chunks.append((gap + kept_t, CROSS, CROSS, lt, (kept_t, half_t + kept_t), True))
    count = len(chunks)
    shard = heads.shape[1]
    tokens = n * rows
    v = lax.axis_index("vocab")
    r = lax.axis_index("rows")
    z, y = lax.div(v, near), lax.rem(v, near)

    barrier = pltpu.get_barrier_semaphore()
    pl.semaphore_signal(barrier, inc=1, device_id={"rows": 1 - r})
    for step in range(1, n):
        pl.semaphore_signal(barrier, inc=1, device_id={"vocab": lax.rem(v + step, n)})

    small = [
        pltpu.make_async_copy(src, dst, small_sem.at[at])
        for at, (src, dst) in enumerate(
            ((th_in, th_ref), (dest_in, dest_ref), (target_in, target_ref), (sh_in, sh_ref))
        )
    ]
    for load in small:
        load.start()
    loads = [
        pltpu.make_async_copy(thead_ref, heads.at[pl.ds(0, wide_t)], head_sem.at[0]),
        pltpu.make_async_copy(shead_ref, heads.at[pl.ds(wide_t, wide_s)], head_sem.at[1]),
    ]
    for load in loads:
        load.start()

    for load in small:
        load.wait()

    lanes = iota((rows, rows), 1)
    place = iota((rows, rows), 0)
    slots = jnp.zeros((rows, rows), jnp.int32)
    for j in range(rows):
        slots = jnp.where(lanes == j, dest_ref[j], slots)
    teacher = th_ref[...]

    def picked(core):
        chosen = jnp.where(slots == core * rows + place, 1.0, 0.0).astype(BF16)
        return jnp.dot(chosen, teacher, preferred_element_type=F32)

    swap_out[...] = stacked(picked(1 - r)).astype(BF16)
    row_at = iota((rows, 128), 0)
    lane_at = iota((rows, 128), 1)
    own_meta = jnp.where(
        lane_at == 2, to_column(weight_ref[...].astype(F32).reshape(1, rows)), 0.0
    )
    for j in range(rows):
        own_meta = jnp.where(
            (row_at == j) & (lane_at == 0), lax.div(target_ref[j], 256).astype(F32),
            jnp.where(
                (row_at == j) & (lane_at == 1), lax.rem(target_ref[j], 256).astype(F32), own_meta
            ),
        )
    kept = picked(r)
    pl.semaphore_wait(barrier, n)

    swap = pltpu.make_async_remote_copy(
        swap_out, swap_in, swap_sem.at[0], swap_sem.at[1], device_id={"rows": 1 - r}
    )
    swap.start()

    def to_all(src, dst, sends, recvs):
        copies = []
        for step in range(1, n):
            copies.append(
                pltpu.make_async_remote_copy(
                    src, dst, sends.at[step - 1], recvs.at[step - 1],
                    device_id={"vocab": lax.rem(v + step, n)},
                )
            )
            copies[-1].start()
        return copies

    student = stacked(sh_ref[...].astype(F32))
    blocks[v, :, :half_s] = student.astype(BF16)
    blocks[v, :, half_s:gap] = jnp.concatenate(
        [own_meta, jnp.zeros_like(own_meta)], axis=0
    ).astype(BF16)

    def piece(source, c):
        return blocks.at[source, :, pl.ds(chunks[c][0], chunks[c][1])]

    def vertical(source, c, up):
        sems = up_sem if up else down_sem
        return pltpu.make_async_remote_copy(
            piece(source, c), piece(source, c), sems.at[source, c], arrive.at[source, c],
            device_id={"vocab": v + near if up else v - near},
        )

    def sideways(source, c, step):
        source_z = lax.div(source, near)
        return pltpu.make_async_remote_copy(
            piece(source, c), piece(source, c), side_sem.at[step - 1, source_z, c],
            arrive.at[source, c],
            device_id={"vocab": z * near + lax.rem(y + step, near)},
        )

    def spread(source, c, up, down, across):
        if up:
            @pl.when(z < far - 1)
            def _():
                vertical(source, c, True).start()
        if down:
            @pl.when(z > 0)
            def _():
                vertical(source, c, False).start()
        if across:
            for step in range(1, near):
                sideways(source, c, step).start()

    def product(c):
        start, _, width, out, tops, _ = chunks[c]
        both = blocks[:, :, start:start + width].astype(F32)
        value = 0.0
        for part in range(2):
            x = both[:, part * rows:(part + 1) * rows].reshape(tokens, width).astype(BF16)
            value += jnp.dot(
                x, heads[tops[part]:tops[part] + width, :], preferred_element_type=F32
            )
        if c == 2:
            value += out[...]
        out[...] = value

    def places(c):
        return [lax.rem(y + step, near) for step in range(near if chunks[c][5] else 1)]

    spread(v, 0, True, True, True)
    swap.wait_recv()
    aligned = stacked(kept) + swap_in[...].astype(F32)
    blocks[v, :, gap:] = aligned.astype(BF16)
    for c in range(1, count):
        spread(v, c, True, True, True)
    for t in range(count + far):
        if t >= 1 and t < count and chunks[t][5]:
            for step in range(1, near):
                beside = z * near + lax.rem(y + step, near)
                sideways(beside, t, step).wait_recv()
                spread(beside, t, True, True, False)
        for d in range(1, far):
            c = t - d
            if 0 <= c < count:
                @pl.when(z >= d)
                def _():
                    for at in places(c):
                        source = (z - d) * near + at
                        vertical(source, c, True).wait_recv()
                        spread(source, c, True, False, not chunks[c][5])

                @pl.when(z + d < far)
                def _():
                    for at in places(c):
                        source = (z + d) * near + at
                        vertical(source, c, False).wait_recv()
                        spread(source, c, False, True, not chunks[c][5])
        c = t - far
        if c >= 0:
            for step in range(1, 1 if chunks[c][5] else near):
                for source_z in range(far):
                    source = source_z * near + lax.rem(y + step, near)
                    sideways(source, c, step).wait_recv()
            if c == 0:
                for load in loads:
                    load.wait()
            product(c)

    info = blocks[:, :, half_s:gap].astype(F32)[:, :rows].reshape(tokens, 128)
    target = (info[:, 0:1] * 256.0 + info[:, 1:2]).astype(jnp.int32) - v * shard
    weight = info[:, 2:3]
    onehot = iota((tokens, shard), 1) == target
    logit_t = capped(lt[...])
    exp_t = jnp.exp(logit_t)
    logit_s = capped(ls[...])
    exp_s = jnp.exp(logit_s)
    sums = (
        jnp.sum(exp_t, axis=1, keepdims=True),
        jnp.sum(exp_t * (logit_t - logit_s), axis=1, keepdims=True),
        jnp.sum(exp_s, axis=1, keepdims=True),
        jnp.sum(jnp.where(onehot, logit_s, 0.0), axis=1, keepdims=True),
    )
    stat_row = iota((8, tokens), 0)
    mine = jnp.zeros((8, tokens), F32)
    for k, column in enumerate(sums):
        mine = jnp.where(stat_row == k, to_row(column), mine)
    stats[v] = mine
    stat_copies = to_all(stats.at[v], stats.at[v], stat_send, stat_recv)
    slope = 1.0 - (logit_s / soft_cap) * (logit_s / soft_cap)
    for copy in stat_copies:
        copy.wait_recv()
    total = jnp.sum(stats[...], axis=0)
    norm_t, cross, norm_s, hit = (total[k:k + 1] for k in range(4))
    zt, zs = to_column(norm_t), to_column(norm_s)
    grad = (
        weight
        * (exp_s * (2.0 / zs) - exp_t * (1.0 / zt) - jnp.where(onehot, 1.0, 0.0))
        * slope
    ).astype(BF16)

    cols = wide_s // 2 // BACK

    def backed(q, part):
        first = wide_t + part * (wide_s // 2) + q * cols
        return lax.dot_general(
            grad, heads[first:first + cols, :], (((1,), (1,)), ((), ())),
            preferred_element_type=F32,
        ).astype(BF16).astype(F32).reshape(n, rows, cols)

    back_copies = []
    for q in range(BACK):
        joined = jnp.concatenate([backed(q, 0), backed(q, 1)], axis=1)
        back_out[:, q] = joined.astype(BF16)
        for step in range(1, n):
            there = lax.rem(v + step, n)
            back_copies.append(
                pltpu.make_async_remote_copy(
                    back_out.at[there, q], back_in.at[step - 1, q],
                    back_send.at[step - 1, q], back_recv.at[step - 1, q],
                    device_id={"vocab": there},
                )
            )
            back_copies[-1].start()

    loss = cross / norm_t - jnp.log(norm_t) + 2.0 * jnp.log(norm_s) - hit
    choose = iota((rows, tokens), 1) == v * rows + iota((rows, tokens), 0)
    loss_ref[...] = to_row(jnp.sum(jnp.where(choose, loss, 0.0), axis=1, keepdims=True))

    k = 0
    for q in range(BACK):
        result = back_out[v, q].astype(F32)
        for step in range(1, n):
            back_copies[k].wait_recv()
            k += 1
            result += back_in[step - 1, q].astype(F32)
        result = jnp.concatenate([result[:rows], result[rows:]], axis=1).astype(BF16)
        hidden_ref[:, q * cols:(q + 1) * cols] = result[:, :cols]
        hidden_ref[:, wide_s // 2 + q * cols:wide_s // 2 + (q + 1) * cols] = result[:, cols:]

    swap.wait_send()
    for copy in stat_copies + back_copies:
        copy.wait_send()
    for c in range(count):
        for d in range(far):
            @pl.when((z >= d) & (z < far - 1))
            def _():
                for at in places(c):
                    vertical((z - d) * near + at, c, True).wait_send()

            @pl.when((z + d < far) & (z > 0))
            def _():
                for at in places(c):
                    vertical((z + d) * near + at, c, False).wait_send()
        if chunks[c][5]:
            for step in range(1, near):
                sideways(v, c, step).wait_send()
        else:
            for source_z in range(far):
                for step in range(1, near):
                    sideways(source_z * near + y, c, step).wait_send()


def hand_on(loss_in, hidden_in, loss_ref, hidden_ref):
    loss_ref[...] = loss_in[...]
    hidden_ref[...] = hidden_in[...]


def local(far, near, teacher_hidden, student_hidden, teacher_head, student_head, dest_slot, targets, token_grad):
    n = far * near
    rows, wide_t = teacher_hidden.shape
    wide_s = student_hidden.shape[1]
    shard = student_head.shape[1]
    tokens = n * rows
    half = (wide_t + wide_s) // 2
    vmem = pl.BlockSpec(memory_space=pltpu.VMEM)
    hbm = pl.BlockSpec(memory_space=pl.ANY)
    dma = pltpu.SemaphoreType.DMA
    loss, hidden = pl.pallas_call(
        functools.partial(kernel, far, near),
        out_shape=(
            jax.ShapeDtypeStruct((1, rows), F32),
            jax.ShapeDtypeStruct((rows, wide_s), BF16),
        ),
        in_specs=[hbm, hbm, hbm, hbm, vmem, hbm, hbm],
        out_specs=(vmem, vmem),
        scratch_shapes=[
            pltpu.VMEM((rows, wide_t), BF16),
            pltpu.VMEM((rows, wide_s), BF16),
            pltpu.SMEM((rows,), jnp.int32),
            pltpu.SMEM((rows,), jnp.int32),
            pltpu.VMEM((wide_t + wide_s, shard), BF16),
            pltpu.VMEM((2 * rows, wide_t // 2), BF16),
            pltpu.VMEM((2 * rows, wide_t // 2), BF16),
            pltpu.VMEM((n, 2 * rows, half + 128), BF16),
            pltpu.VMEM((n, 8, tokens), F32),
            pltpu.VMEM((tokens, shard), F32),
            pltpu.VMEM((tokens, shard), F32),
            pltpu.VMEM((n, BACK, 2 * rows, wide_s // 2 // BACK), BF16),
            pltpu.VMEM((n - 1, BACK, 2 * rows, wide_s // 2 // BACK), BF16),
            dma((4,)),
            dma((2,)),
            dma((2,)),
            dma((n, 3)),
            dma((n, 3)),
            dma((n, 3)),
            dma((near - 1, far, 3)),
            dma((n - 1,)),
            dma((n - 1,)),
            dma((n - 1, BACK)),
            dma((n - 1, BACK)),
        ],
        compiler_params=pltpu.CompilerParams(
            collective_id=0, has_side_effects=True, vmem_limit_bytes=56 * 2**20
        ),
    )(teacher_hidden, student_hidden, dest_slot, targets, token_grad, teacher_head, student_head)
    loss, hidden = pl.pallas_call(
        hand_on,
        out_shape=(jax.ShapeDtypeStruct((1, rows), F32), jax.ShapeDtypeStruct((rows, wide_s), BF16)),
        in_specs=[vmem, vmem],
        out_specs=(vmem, vmem),
    )(loss, hidden)
    return loss.reshape(rows), hidden


def solution(mesh):
    n = mesh.shape["vocab"]
    near = 1 << ((n.bit_length() - 1) // 2)
    far = n // near
    by_token = P(("groups", "vocab", "rows"))
    by_row = P(("groups", "vocab", "rows"), None)
    by_vocab = P(None, "vocab")
    return jax.shard_map(
        functools.partial(local, far, near),
        mesh=mesh,
        in_specs=(by_row, by_row, by_vocab, by_vocab, by_token, by_token, by_token),
        out_specs=(by_token, by_row),
        check_vma=False,
    )
```

```python
import functools

import jax
import jax.numpy as jnp
from jax import lax
from jax.experimental import pallas as pl
from jax.experimental.pallas import tpu as pltpu
from jax.sharding import PartitionSpec as P

soft_cap = 30.0
CROSS = 768
BACK = 1
F32 = jnp.float32
BF16 = jnp.bfloat16


def capped(values):
    return soft_cap * jnp.tanh(values / soft_cap)


def iota(shape, dim):
    return lax.broadcasted_iota(jnp.int32, shape, dim)


def to_row(column):
    size = column.shape[0]
    eye = iota((size, size), 0) == iota((size, size), 1)
    return jnp.sum(jnp.where(eye, column, 0.0), axis=0, keepdims=True)


def to_column(row):
    size = row.shape[1]
    eye = iota((size, size), 0) == iota((size, size), 1)
    return jnp.sum(jnp.where(eye, row, 0.0), axis=1, keepdims=True)


def stacked(values):
    half = values.shape[1] // 2
    return jnp.concatenate([values[:, :half], values[:, half:]], axis=0)


def kernel(
    far, near,
    th_in, sh_in, dest_in, target_in, weight_ref, thead_ref, shead_ref,
    loss_ref, hidden_ref,
    th_ref, sh_ref, dest_ref, target_ref, heads, swap_out, swap_in, blocks, stats, lt, ls, back_out, back_in,
    small_sem, head_sem, swap_sem, arrive, up_sem, down_sem, side_sem,
    stat_send, stat_recv, back_send, back_recv,
):
    n = far * near
    rows, wide_t = th_ref.shape
    wide_s = sh_ref.shape[1]
    half_s, half_t = wide_s // 2, wide_t // 2
    gap = half_s + 128
    kept_t = half_t - CROSS
    chunks = [
        (0, gap, half_s, ls, (wide_t, wide_t + half_s), False),
        (gap, kept_t, kept_t, lt, (0, half_t), False),
    ]
    if CROSS:
        chunks.append((gap + kept_t, CROSS, CROSS, lt, (kept_t, half_t + kept_t), True))
    count = len(chunks)
    shard = heads.shape[1]
    tokens = n * rows
    v = lax.axis_index("vocab")
    r = lax.axis_index("rows")
    z, y = lax.div(v, near), lax.rem(v, near)

    barrier = pltpu.get_barrier_semaphore()
    pl.semaphore_signal(barrier, inc=1, device_id={"rows": 1 - r})
    for step in range(1, n):
        pl.semaphore_signal(barrier, inc=1, device_id={"vocab": lax.rem(v + step, n)})

    small = [
        pltpu.make_async_copy(src, dst, small_sem.at[at])
        for at, (src, dst) in enumerate(
            ((th_in, th_ref), (dest_in, dest_ref), (target_in, target_ref), (sh_in, sh_ref))
        )
    ]
    for load in small:
        load.start()
    loads = [
        pltpu.make_async_copy(thead_ref, heads.at[pl.ds(0, wide_t)], head_sem.at[0]),
        pltpu.make_async_copy(shead_ref, heads.at[pl.ds(wide_t, wide_s)], head_sem.at[1]),
    ]
    for load in loads:
        load.start()

    for load in small:
        load.wait()

    lanes = iota((rows, rows), 1)
    place = iota((rows, rows), 0)
    slots = jnp.zeros((rows, rows), jnp.int32)
    for j in range(rows):
        slots = jnp.where(lanes == j, dest_ref[j], slots)
    teacher = th_ref[...]

    def picked(core):
        chosen = jnp.where(slots == core * rows + place, 1.0, 0.0).astype(BF16)
        return jnp.dot(chosen, teacher, preferred_element_type=F32)

    swap_out[...] = stacked(picked(1 - r)).astype(BF16)
    row_at = iota((rows, 128), 0)
    lane_at = iota((rows, 128), 1)
    own_meta = jnp.where(
        lane_at == 2, to_column(weight_ref[...].astype(F32).reshape(1, rows)), 0.0
    )
    for j in range(rows):
        own_meta = jnp.where(
            (row_at == j) & (lane_at == 0), lax.div(target_ref[j], 256).astype(F32),
            jnp.where(
                (row_at == j) & (lane_at == 1), lax.rem(target_ref[j], 256).astype(F32), own_meta
            ),
        )
    kept = picked(r)
    pl.semaphore_wait(barrier, n)

    swap = pltpu.make_async_remote_copy(
        swap_out, swap_in, swap_sem.at[0], swap_sem.at[1], device_id={"rows": 1 - r}
    )
    swap.start()

    order = list(range(1, n))

    def to_all(src, dst, sends, recvs):
        copies = []
        for step in order:
            copies.append(
                pltpu.make_async_remote_copy(
                    src, dst, sends.at[step - 1], recvs.at[step - 1],
                    device_id={"vocab": lax.rem(v + step, n)},
                )
            )
            copies[-1].start()
        return copies

    student = stacked(sh_ref[...].astype(F32))
    blocks[v, :, :half_s] = student.astype(BF16)
    blocks[v, :, half_s:gap] = jnp.concatenate(
        [own_meta, jnp.zeros_like(own_meta)], axis=0
    ).astype(BF16)

    def piece(source, c):
        return blocks.at[source, :, pl.ds(chunks[c][0], chunks[c][1])]

    def vertical(source, c, up):
        sems = up_sem if up else down_sem
        return pltpu.make_async_remote_copy(
            piece(source, c), piece(source, c), sems.at[source, c], arrive.at[source, c],
            device_id={"vocab": v + near if up else v - near},
        )

    def sideways(source, c, step):
        source_z = lax.div(source, near)
        return pltpu.make_async_remote_copy(
            piece(source, c), piece(source, c), side_sem.at[step - 1, source_z, c],
            arrive.at[source, c],
            device_id={"vocab": z * near + lax.rem(y + step, near)},
        )

    def spread(source, c, up, down, across):
        if up:
            @pl.when(z < far - 1)
            def _():
                vertical(source, c, True).start()
        if down:
            @pl.when(z > 0)
            def _():
                vertical(source, c, False).start()
        if across:
            for step in range(1, near):
                sideways(source, c, step).start()

    def product(c):
        start, _, width, out, tops, _ = chunks[c]
        both = blocks[:, :, start:start + width].astype(F32)
        value = 0.0
        for part in range(2):
            x = both[:, part * rows:(part + 1) * rows].reshape(tokens, width).astype(BF16)
            value += jnp.dot(
                x, heads[tops[part]:tops[part] + width, :], preferred_element_type=F32
            )
        if c == 2:
            value += out[...]
        out[...] = value

    def places(c):
        return [lax.rem(y + step, near) for step in range(near if chunks[c][5] else 1)]

    spread(v, 0, True, True, True)
    swap.wait_recv()
    aligned = stacked(kept) + swap_in[...].astype(F32)
    blocks[v, :, gap:] = aligned.astype(BF16)
    for c in range(1, count):
        spread(v, c, True, True, True)
    for t in range(count + far):
        if t >= 1 and t < count and chunks[t][5]:
            for step in range(1, near):
                beside = z * near + lax.rem(y + step, near)
                sideways(beside, t, step).wait_recv()
                spread(beside, t, True, True, False)
        for d in range(1, far):
            c = t - d
            if 0 <= c < count:
                @pl.when(z >= d)
                def _():
                    for at in places(c):
                        source = (z - d) * near + at
                        vertical(source, c, True).wait_recv()
                        spread(source, c, True, False, not chunks[c][5])

                @pl.when(z + d < far)
                def _():
                    for at in places(c):
                        source = (z + d) * near + at
                        vertical(source, c, False).wait_recv()
                        spread(source, c, False, True, not chunks[c][5])
        c = t - far
        if c >= 0:
            for step in range(1, 1 if chunks[c][5] else near):
                for source_z in range(far):
                    source = source_z * near + lax.rem(y + step, near)
                    sideways(source, c, step).wait_recv()
            if c == 0:
                for load in loads:
                    load.wait()
            product(c)
            if c == 0:
                info = blocks[:, :, half_s:gap].astype(F32)[:, :rows].reshape(tokens, 128)
                target = (info[:, 0:1] * 256.0 + info[:, 1:2]).astype(jnp.int32) - v * shard
                weight = info[:, 2:3]
                onehot = iota((tokens, shard), 1) == target
                logit_s = capped(ls[...])
                exp_s = jnp.exp(logit_s)
                sum_s = jnp.sum(exp_s, axis=1, keepdims=True)
                sum_hit = jnp.sum(jnp.where(onehot, logit_s, 0.0), axis=1, keepdims=True)
                slope = 1.0 - (logit_s / soft_cap) * (logit_s / soft_cap)

    logit_t = capped(lt[...])
    exp_t = jnp.exp(logit_t)
    sums = (
        jnp.sum(exp_t, axis=1, keepdims=True),
        jnp.sum(exp_t * (logit_t - logit_s), axis=1, keepdims=True),
        sum_s,
        sum_hit,
    )
    stat_row = iota((8, tokens), 0)
    mine = jnp.zeros((8, tokens), F32)
    for k, column in enumerate(sums):
        mine = jnp.where(stat_row == k, to_row(column), mine)
    stats[v] = mine
    stat_copies = to_all(stats.at[v], stats.at[v], stat_send, stat_recv)
    scale = weight * slope
    grad_s, grad_t, grad_hit = 2.0 * scale * exp_s, scale * exp_t, jnp.where(onehot, scale, 0.0)
    for copy in stat_copies:
        copy.wait_recv()
    total = jnp.sum(stats[...], axis=0)
    norm_t, cross, norm_s, hit = (total[k:k + 1] for k in range(4))
    zt, zs = to_column(norm_t), to_column(norm_s)
    grad = (grad_s * (1.0 / zs) - grad_t * (1.0 / zt) - grad_hit).astype(BF16)

    cols = wide_s // 2 // BACK

    def backed(q, part):
        first = wide_t + part * (wide_s // 2) + q * cols
        return lax.dot_general(
            grad, heads[first:first + cols, :], (((1,), (1,)), ((), ())),
            preferred_element_type=F32,
        ).astype(BF16).astype(F32).reshape(n, rows, cols)

    back_copies = []
    for q in range(BACK):
        joined = jnp.concatenate([backed(q, 0), backed(q, 1)], axis=1)
        back_out[:, q] = joined.astype(BF16)
        for step in order:
            there = lax.rem(v + step, n)
            back_copies.append(
                pltpu.make_async_remote_copy(
                    back_out.at[there, q], back_in.at[step - 1, q],
                    back_send.at[step - 1, q], back_recv.at[step - 1, q],
                    device_id={"vocab": there},
                )
            )
            back_copies[-1].start()

    loss = cross / norm_t - jnp.log(norm_t) + 2.0 * jnp.log(norm_s) - hit
    choose = iota((rows, tokens), 1) == v * rows + iota((rows, tokens), 0)
    loss_ref[...] = to_row(jnp.sum(jnp.where(choose, loss, 0.0), axis=1, keepdims=True))

    k = 0
    for q in range(BACK):
        result = back_out[v, q].astype(F32)
        for step in order:
            back_copies[k].wait_recv()
            k += 1
            result += back_in[step - 1, q].astype(F32)
        result = jnp.concatenate([result[:rows], result[rows:]], axis=1).astype(BF16)
        hidden_ref[:, q * cols:(q + 1) * cols] = result[:, :cols]
        hidden_ref[:, wide_s // 2 + q * cols:wide_s // 2 + (q + 1) * cols] = result[:, cols:]

    swap.wait_send()
    for copy in stat_copies + back_copies:
        copy.wait_send()
    for c in range(count):
        for d in range(far):
            @pl.when((z >= d) & (z < far - 1))
            def _():
                for at in places(c):
                    vertical((z - d) * near + at, c, True).wait_send()

            @pl.when((z + d < far) & (z > 0))
            def _():
                for at in places(c):
                    vertical((z + d) * near + at, c, False).wait_send()
        if chunks[c][5]:
            for step in range(1, near):
                sideways(v, c, step).wait_send()
        else:
            for source_z in range(far):
                for step in range(1, near):
                    sideways(source_z * near + y, c, step).wait_send()


def hand_on(loss_in, hidden_in, loss_ref, hidden_ref):
    loss_ref[...] = loss_in[...]
    hidden_ref[...] = hidden_in[...]


def local(far, near, teacher_hidden, student_hidden, teacher_head, student_head, dest_slot, targets, token_grad):
    n = far * near
    rows, wide_t = teacher_hidden.shape
    wide_s = student_hidden.shape[1]
    shard = student_head.shape[1]
    tokens = n * rows
    half = (wide_t + wide_s) // 2
    vmem = pl.BlockSpec(memory_space=pltpu.VMEM)
    hbm = pl.BlockSpec(memory_space=pl.ANY)
    dma = pltpu.SemaphoreType.DMA
    loss, hidden = pl.pallas_call(
        functools.partial(kernel, far, near),
        out_shape=(
            jax.ShapeDtypeStruct((1, rows), F32),
            jax.ShapeDtypeStruct((rows, wide_s), BF16),
        ),
        in_specs=[hbm, hbm, hbm, hbm, vmem, hbm, hbm],
        out_specs=(vmem, vmem),
        scratch_shapes=[
            pltpu.VMEM((rows, wide_t), BF16),
            pltpu.VMEM((rows, wide_s), BF16),
            pltpu.SMEM((rows,), jnp.int32),
            pltpu.SMEM((rows,), jnp.int32),
            pltpu.VMEM((wide_t + wide_s, shard), BF16),
            pltpu.VMEM((2 * rows, wide_t // 2), BF16),
            pltpu.VMEM((2 * rows, wide_t // 2), BF16),
            pltpu.VMEM((n, 2 * rows, half + 128), BF16),
            pltpu.VMEM((n, 8, tokens), F32),
            pltpu.VMEM((tokens, shard), F32),
            pltpu.VMEM((tokens, shard), F32),
            pltpu.VMEM((n, BACK, 2 * rows, wide_s // 2 // BACK), BF16),
            pltpu.VMEM((n - 1, BACK, 2 * rows, wide_s // 2 // BACK), BF16),
            dma((4,)),
            dma((2,)),
            dma((2,)),
            dma((n, 3)),
            dma((n, 3)),
            dma((n, 3)),
            dma((near - 1, far, 3)),
            dma((n - 1,)),
            dma((n - 1,)),
            dma((n - 1, BACK)),
            dma((n - 1, BACK)),
        ],
        compiler_params=pltpu.CompilerParams(
            collective_id=0, has_side_effects=True, vmem_limit_bytes=56 * 2**20
        ),
    )(teacher_hidden, student_hidden, dest_slot, targets, token_grad, teacher_head, student_head)
    loss, hidden = pl.pallas_call(
        hand_on,
        out_shape=(jax.ShapeDtypeStruct((1, rows), F32), jax.ShapeDtypeStruct((rows, wide_s), BF16)),
        in_specs=[vmem, vmem],
        out_specs=(vmem, vmem),
    )(loss, hidden)
    return loss.reshape(rows), hidden


def solution(mesh):
    n = mesh.shape["vocab"]
    near = 1 << ((n.bit_length() - 1) // 2)
    far = n // near
    by_token = P(("groups", "vocab", "rows"))
    by_row = P(("groups", "vocab", "rows"), None)
    by_vocab = P(None, "vocab")
    return jax.shard_map(
        functools.partial(local, far, near),
        mesh=mesh,
        in_specs=(by_row, by_row, by_vocab, by_vocab, by_token, by_token, by_token),
        out_specs=(by_token, by_row),
        check_vma=False,
    )
```
